32 devices in a mesh: freq: 2 (over y), mid: 4 (over z), off: 4 (over x, core).
Axes of the slice: x: 2, y: 2, z: 4, core: 2. Of those that a mesh axis runs over, the one named last changes fastest.
Arguments:
- observed: bfloat16 [4, 8192, 8192], P('freq', 'mid', 'off'), parts along dimension 0, may hold values from -6 to 6
- trace_mask: int32 [8192, 8192], P('mid', 'off'), may hold values 0 or 1
- left_factor: bfloat16 [4, 8192, 256], P('freq', ('mid', 'off')), parts along dimension 0, may hold values from -1.5 to 1.5
- right_factor: bfloat16 [4, 8192, 256], P('freq', ('off', 'mid')), parts along dimension 0, may hold values from -1.5 to 1.5
Outputs:
- left_next: float32 [4, 8192, 256], P('freq', ('mid', 'off')), parts along dimension 0
- right_next: float32 [4, 8192, 256], P('freq', ('off', 'mid')), parts along dimension 0
The draws below stay inside these ranges and needn't reach their ends.
There are 2 independent parts, one for each index of `freq`. The reference program is written for one: setup_inputs(seed, part) draws one part's arguments, and reference() takes and returns one part's arrays. A program takes and returns all parts, laid end to end along the dimension named above; an argument that names none is the same for every part. Nothing has to cross between parts.
All inputs are finite; a program needn't handle non-finite values. No bound on the sum of `trace_mask` on one device may be relied on, other than what follows from the above.
Results may differ from the reference program's by a relative error of at most 0.0011.
Values may be sent and summed in bfloat16 or wider, within the bound.
A program may use at most 192 MiB of HBM per device.

```python
import math
import jax
import jax.numpy as jnp

N = 8192
K = 256


def plant(result, key, smallest, high):
    extent = result.shape
    index_at = [jax.random.randint(jax.random.fold_in(key, axis), (), 0, extent[axis]) for axis in range(len(extent))]
    result = result.at[tuple(index_at)].set(smallest)
    longest = extent.index(max(extent))
    index_at[longest] = (index_at[longest] + 1) % extent[longest]
    return result.at[tuple(index_at)].set(high)


def steps_of(rng, extent, shards, low, largest):
    level, own = 1.0, jax.random.fold_in(rng, 6)
    for dim, parts in shards:
        draws = jnp.exp(jax.random.uniform(jax.random.fold_in(own, dim), (parts,), jnp.float32, low / len(shards), largest / len(shards)))
        level = level * jnp.repeat(draws, extent[dim] // parts).reshape([-1 if axis == dim else 1 for axis in range(len(extent))])
    return level


def gaussian(key, extent, width, bound, pieces=(), dtype=jnp.bfloat16):
    array = jax.random.normal(key, extent, jnp.float32) * width
    if len(pieces) > 0:
        array = steps_of(key, extent, pieces, -0.22, 0.18) * array
    return jnp.clip(array, min=-bound, max=bound).astype(dtype)


def setup_inputs(seed: int = 0, part: int = 0) -> dict:
    key_of = jax.random.split(jax.random.key(seed), 5)
    part_keys = jax.random.split(jax.random.fold_in(key_of[4], part), 5)
    observed = gaussian(part_keys[0], (2, N, N), 1.0, 6.0, ((1, 4), (2, 4)))
    trace_mask = plant((jax.random.randint(key_of[1], (N, N), 0, 5) < 2).astype(jnp.int32), jax.random.fold_in(key_of[1], 1), 0, 1)
    left_factor = gaussian(part_keys[2], (2, N, K), 0.25, 1.5, ((1, 16),))
    right_factor = gaussian(part_keys[3], (2, N, K), 0.25, 1.5, ((1, 16),))
    return dict(observed=observed, trace_mask=trace_mask, left_factor=left_factor, right_factor=right_factor)


def mm(a, b):
    return jnp.dot(a, b, preferred_element_type=jnp.float32)

def reference(observed, trace_mask, left_factor, right_factor):
    left_re, left_im = (left_factor[0], left_factor[1])
    right_re, right_im = (right_factor[0], right_factor[1])
    keep = trace_mask.astype(jnp.float32)
    real_part = mm(left_re, right_re.T) + mm(left_im, right_im.T)
    imag_part = mm(left_im, right_re.T) - mm(left_re, right_im.T)
    miss_re = (keep * (real_part - observed[0].astype(jnp.float32))).astype(jnp.bfloat16)
    miss_im = (keep * (imag_part - observed[1].astype(jnp.float32))).astype(jnp.bfloat16)
    grad_left = jnp.stack([mm(miss_re, right_re) - mm(miss_im, right_im), mm(miss_re, right_im) + mm(miss_im, right_re)])
    grad_right = jnp.stack([mm(miss_re.T, left_re) + mm(miss_im.T, left_im), mm(miss_re.T, left_im) - mm(miss_im.T, left_re)])
    step_size = 2.0 / math.sqrt(N)
    left_next = left_factor.astype(jnp.float32) - step_size * grad_left
    right_next = right_factor.astype(jnp.float32) - step_size * grad_right
    return (left_next, right_next)
```

```python
import math

import jax
import jax.numpy as jnp
from jax import lax
from jax.experimental import pallas as pl
from jax.experimental.pallas import tpu as pltpu
from jax.sharding import PartitionSpec as P

N = 8192
STEP = 2.0 / math.sqrt(N)
LINK = jnp.int16
LEVELS = 32000.0
PIECES = 4
MESH = pl.DeviceIdType.MESH


def outer_rows(first, second):
    return jnp.einsum("ik,jk->ij", first, second, preferred_element_type=jnp.float32)


def inner_rows(first, second):
    return jnp.einsum("ij,jk->ik", first, second, preferred_element_type=jnp.float32)


def inner_cols(first, second):
    return jnp.einsum("ij,ik->jk", first, second, preferred_element_type=jnp.float32)


def plain_device(observed, trace_mask, left_factor, right_factor):
    left = lax.all_gather(left_factor, "off", axis=1, tiled=True)
    keep = trace_mask.astype(jnp.float32)
    right = lax.all_gather(right_factor, "mid", axis=1, tiled=True)
    real_part = outer_rows(left[0], right[0]) + outer_rows(left[1], right[1])
    imag_part = outer_rows(left[1], right[0]) - outer_rows(left[0], right[1])
    miss_re = (keep * (real_part - observed[0].astype(jnp.float32))).astype(jnp.bfloat16)
    miss_im = (keep * (imag_part - observed[1].astype(jnp.float32))).astype(jnp.bfloat16)
    grad_left = jnp.stack(
        [
            inner_rows(miss_re, right[0]) - inner_rows(miss_im, right[1]),
            inner_rows(miss_re, right[1]) + inner_rows(miss_im, right[0]),
        ]
    )
    grad_right = jnp.stack(
        [
            inner_cols(miss_re, left[0]) + inner_cols(miss_im, left[1]),
            inner_cols(miss_re, left[1]) - inner_cols(miss_im, left[0]),
        ]
    )
    right_share = lax.psum_scatter(grad_right, "mid", scatter_dimension=1, tiled=True)
    left_share = lax.psum_scatter(grad_left, "off", scatter_dimension=1, tiled=True)
    left_next = left_factor.astype(jnp.float32) - STEP * left_share
    right_next = right_factor.astype(jnp.float32) - STEP * right_share
    return (left_next, right_next)


def coded(value):
    top = jnp.maximum(jnp.max(jnp.abs(value), axis=0, keepdims=True), 1e-30)
    levels = jnp.floor(value * (LEVELS / top) + 0.5)
    return levels.astype(jnp.int32).astype(LINK), top * (1.0 / LEVELS)


class Both:
    def __init__(self, *copies):
        self.copies = copies

    def start(self):
        for c in self.copies:
            c.start()

    def wait_recv(self):
        for c in self.copies:
            c.wait_recv()

    def wait_send(self):
        for c in self.copies:
            c.wait_send()


def kernel(
    n, rb, k, tr,
    obs_hbm, mask_hbm, left_hbm, right_hbm,
    gl_out, gr_out,
    lfull, rcat, rbig, lt, obs, mask, gl, gr,
    zsend, zrecv, asend, arecv, bsend, brecv,
    zsend_s, zrecv_s, asend_s, arecv_s, bsend_s, brecv_s,
    in_sem, obs_sem, mask_sem,
    g_send_r, g_send_l, g_recv,
    l_send, l_recv,
    z_send_sem, z_recv_sem,
    a_send_sem, a_recv_sem, b_send_sem, b_recv_sem,
    z_send_sem_s, z_recv_sem_s, a_send_sem_s, a_recv_sem_s, b_send_sem_s, b_recv_sem_s,
):
    me = lax.axis_index("mid")
    off = lax.axis_index("off")
    sib = off + 1 - 2 * lax.rem(off, 2)
    cross = lax.rem(off + 2, 4)
    diag = lax.rem(sib + 2, 4)
    lo = jnp.minimum(me, n - 1 - me)
    has_l = me > 0
    has_r = me < n - 1
    piece = 2 * k // PIECES
    tiles = rb // tr

    def block_at(j):
        near = (j + 1) // 2
        up = lax.rem(j, 2) == 1
        paired = jnp.where(up, me + near, me - near)
        far = j - lo
        single = jnp.where(me < n - 1 - me, me + far, me - far)
        return jnp.where(j <= 2 * lo, paired, single)

    def row_block(q):
        return jnp.where(q == 0, off, jnp.where(q == 1, sib, jnp.where(q == 2, cross, diag)))

    def obs_copy(j):
        b = block_at(j)
        cols = pl.ds(pl.multiple_of(b * rb, rb), rb)
        slot = lax.rem(j, 2)
        return (
            pltpu.make_async_copy(obs_hbm.at[:, :, cols], obs.at[slot], obs_sem.at[slot]),
            pltpu.make_async_copy(mask_hbm.at[:, cols], mask.at[slot], mask_sem.at[slot]),
        )

    def gather_right(b):
        return pltpu.make_async_remote_copy(
            src_ref=rcat.at[b], dst_ref=rcat.at[b], send_sem=g_send_r.at[b], recv_sem=g_recv.at[b],
            device_id={"mid": jnp.minimum(me + 1, n - 1)}, device_id_type=MESH)

    def gather_left(b):
        return pltpu.make_async_remote_copy(
            src_ref=rcat.at[b], dst_ref=rcat.at[b], send_sem=g_send_l.at[b], recv_sem=g_recv.at[b],
            device_id={"mid": jnp.maximum(me - 1, 0)}, device_id_type=MESH)

    def left_copy(block, to, which):
        return pltpu.make_async_remote_copy(
            src_ref=lfull.at[block], dst_ref=lfull.at[block],
            send_sem=l_send.at[which], recv_sem=l_recv.at[which],
            device_id={"off": to}, device_id_type=MESH)

    def arrive(b):
        @pl.when(b < me)
        def _():
            gather_right(b).wait_recv()

            @pl.when(has_r)
            def _():
                gather_right(b).start()

        @pl.when(b > me)
        def _():
            gather_left(b).wait_recv()

            @pl.when(has_l)
            def _():
                gather_left(b).start()

    def sum_right(t, p):
        to = jnp.minimum(me + 1, n - 1)
        return Both(
            pltpu.make_async_remote_copy(
                src_ref=zsend.at[t, p], dst_ref=zrecv.at[t, p],
                send_sem=z_send_sem.at[t, p], recv_sem=z_recv_sem.at[t, p],
                device_id={"mid": to}, device_id_type=MESH),
            pltpu.make_async_remote_copy(
                src_ref=zsend_s.at[t, p], dst_ref=zrecv_s.at[t, p],
                send_sem=z_send_sem_s.at[t, p], recv_sem=z_recv_sem_s.at[t, p],
                device_id={"mid": to}, device_id_type=MESH))

    def sum_left(t, p):
        to = jnp.maximum(me - 1, 0)
        slot = jnp.where(t == me - 1, n, t)
        return Both(
            pltpu.make_async_remote_copy(
                src_ref=zsend.at[t, p], dst_ref=zrecv.at[slot, p],
                send_sem=z_send_sem.at[t, p], recv_sem=z_recv_sem.at[slot, p],
                device_id={"mid": to}, device_id_type=MESH),
            pltpu.make_async_remote_copy(
                src_ref=zsend_s.at[t, p], dst_ref=zrecv_s.at[slot, p],
                send_sem=z_send_sem_s.at[t, p], recv_sem=z_recv_sem_s.at[slot, p],
                device_id={"mid": to}, device_id_type=MESH))

    def sum_arrived(slot, p):
        return Both(
            pltpu.make_async_remote_copy(
                src_ref=zrecv.at[slot, p], dst_ref=zrecv.at[slot, p],
                send_sem=z_send_sem.at[0, p], recv_sem=z_recv_sem.at[slot, p],
                device_id={"off": sib}, device_id_type=MESH),
            pltpu.make_async_remote_copy(
                src_ref=zrecv_s.at[slot, p], dst_ref=zrecv_s.at[slot, p],
                send_sem=z_send_sem_s.at[0, p], recv_sem=z_recv_sem_s.at[slot, p],
                device_id={"off": sib}, device_id_type=MESH))

    def a_copy(which):
        return Both(
            pltpu.make_async_remote_copy(
                src_ref=asend.at[which], dst_ref=arecv.at[which],
                send_sem=a_send_sem.at[which], recv_sem=a_recv_sem.at[which],
                device_id={"off": sib}, device_id_type=MESH),
            pltpu.make_async_remote_copy(
                src_ref=asend_s.at[which], dst_ref=arecv_s.at[which],
                send_sem=a_send_sem_s.at[which], recv_sem=a_recv_sem_s.at[which],
                device_id={"off": sib}, device_id_type=MESH))

    def b_copy():
        return Both(
            pltpu.make_async_remote_copy(
                src_ref=bsend, dst_ref=brecv, send_sem=b_send_sem, recv_sem=b_recv_sem,
                device_id={"off": cross}, device_id_type=MESH),
            pltpu.make_async_remote_copy(
                src_ref=bsend_s, dst_ref=brecv_s, send_sem=b_send_sem_s, recv_sem=b_recv_sem_s,
                device_id={"off": cross}, device_id_type=MESH))

    def z_received(slot, p):
        return zrecv[slot, p].astype(jnp.float32) * zrecv_s[slot, p]

    def z_put(t, p, value):
        zsend[t, p], zsend_s[t, p] = coded(value)

    own = [
        pltpu.make_async_copy(left_hbm.at[0], lfull.at[off, :, 0:k], in_sem.at[0]),
        pltpu.make_async_copy(left_hbm.at[1], lfull.at[off, :, k:2 * k], in_sem.at[1]),
        pltpu.make_async_copy(right_hbm.at[0], rcat.at[me, :, 0:k], in_sem.at[2]),
        pltpu.make_async_copy(right_hbm.at[1], rcat.at[me, :, k:2 * k], in_sem.at[3]),
    ]
    for c in own:
        c.start()
    for c in obs_copy(0):
        c.start()

    barrier = pltpu.get_barrier_semaphore()
    for to in (sib, cross):
        pl.semaphore_signal(barrier, inc=1, device_id={"off": to}, device_id_type=MESH)

    @pl.when(has_l)
    def _():
        pl.semaphore_signal(barrier, inc=1, device_id={"mid": me - 1}, device_id_type=MESH)

    @pl.when(has_r)
    def _():
        pl.semaphore_signal(barrier, inc=1, device_id={"mid": me + 1}, device_id_type=MESH)

    pl.semaphore_wait(barrier, 2 + jnp.where(has_l, 1, 0) + jnp.where(has_r, 1, 0))

    for c in own:
        c.wait()

    left_copy(off, cross, 1).start()
    left_copy(off, sib, 0).start()

    @pl.when(has_r)
    def _():
        gather_right(me).start()

    @pl.when(has_l)
    def _():
        gather_left(me).start()

    gl[...] = jnp.zeros_like(gl)

    def step(j, carry):
        b = block_at(j)
        slot = lax.rem(j, 2)

        @pl.when(j < n - 1)
        def _():
            for c in obs_copy(j + 1):
                c.start()

        rbig[0:rb, :] = rcat[b]
        rbig[rb:2 * rb, 0:k] = -rcat[b, :, k:2 * k]
        rbig[rb:2 * rb, k:2 * k] = rcat[b, :, 0:k]
        gr[b] = jnp.zeros(gr.shape[1:], jnp.float32)
        for c in obs_copy(j):
            c.wait()

        def rows(i, carry):
            q_of = i // tiles
            t = lax.rem(i, tiles)
            q = jnp.where(j == n - 1, 3 - q_of, q_of)
            block = row_block(q)

            @pl.when(jnp.logical_and(j == 0, t == 0))
            def _():
                @pl.when(q == 1)
                def _():
                    left_copy(sib, sib, 0).wait_recv()

                @pl.when(q == 2)
                def _():
                    left_copy(cross, cross, 1).wait_recv()
                    left_copy(cross, sib, 2).start()

                @pl.when(q == 3)
                def _():
                    left_copy(diag, sib, 2).wait_recv()

            @pl.when(jnp.logical_and(j < n - 1, i == 2 * tiles))
            def _():
                nxt = j + 1
                pair = jnp.logical_and(nxt <= 2 * lo, lax.rem(nxt, 2) == 1)

                @pl.when(pair)
                def _():
                    near = (nxt + 1) // 2
                    arrive(me + near)
                    arrive(me - near)

                @pl.when(nxt > 2 * lo)
                def _():
                    arrive(block_at(nxt))

            at = pl.ds(pl.multiple_of(t * tr, tr), tr)
            row_at = pl.ds(pl.multiple_of(block * rb + t * tr, tr), tr)
            lrows = lfull[block, at, :]

            @pl.when(j == 0)
            def _():
                turned = lrows.astype(jnp.float32).T.astype(jnp.bfloat16)
                lt[block * tiles + t, :, 0:tr] = turned
                lt[block * tiles + t, 0:k, tr:2 * tr] = turned[k:2 * k]
                lt[block * tiles + t, k:2 * k, tr:2 * tr] = -turned[0:k]

            pred = lax.dot_general(
                lrows, rbig[...], (((1,), (1,)), ((), ())), preferred_element_type=jnp.float32)
            keep = mask[slot, row_at, :] != 0
            miss_re = jnp.where(
                keep, pred[:, 0:rb] - obs[slot, 0, row_at, :].astype(jnp.float32), 0.0
            ).astype(jnp.bfloat16)
            miss_im = jnp.where(
                keep, pred[:, rb:2 * rb] - obs[slot, 1, row_at, :].astype(jnp.float32), 0.0
            ).astype(jnp.bfloat16)
            gl[block, at, :] += jnp.dot(
                jnp.concatenate([miss_re, miss_im], axis=1), rbig[...],
                preferred_element_type=jnp.float32)
            gr[b] += jnp.dot(
                lt[block * tiles + t], jnp.concatenate([miss_re, miss_im], axis=0),
                preferred_element_type=jnp.float32)

            @pl.when(jnp.logical_and(j == n - 1, t == tiles - 1))
            def _():
                @pl.when(q == 3)
                def _():
                    asend[0], asend_s[0] = coded(gl[diag])
                    a_copy(0).start()

                @pl.when(q == 1)
                def _():
                    asend[1], asend_s[1] = coded(gl[sib])
                    a_copy(1).start()

            return carry

        lax.fori_loop(0, 4 * tiles, rows, 0)

        @pl.when(jnp.logical_and(me == 0, b > me))
        def _():
            for p in range(PIECES):
                z_put(b, p, gr[b, p * piece:(p + 1) * piece, :])
                sum_right(b, p).start()

        @pl.when(jnp.logical_and(me == n - 1, b < me))
        def _():
            for p in range(PIECES):
                z_put(b, p, gr[b, p * piece:(p + 1) * piece, :])
                sum_left(b, p).start()

        return carry

    lax.fori_loop(0, n, step, 0)

    a_copy(0).wait_recv()
    bsend[...], bsend_s[...] = coded(gl[cross] + arecv[0].astype(jnp.float32) * arecv_s[0])
    b_copy().start()

    def pass_on(tau, carry):
        right_t = tau - me
        left_t = 2 * (n - 1) - me - tau

        @pl.when((me > 0) & (right_t > me) & (right_t < n))
        def _():
            for p in range(PIECES):
                sum_arrived(right_t, p).wait_recv()
                z_put(right_t, p, gr[right_t, p * piece:(p + 1) * piece, :] + z_received(right_t, p))
                sum_right(right_t, p).start()

        @pl.when((me < n - 1) & (left_t < me) & (left_t >= 0))
        def _():
            for p in range(PIECES):
                sum_arrived(left_t, p).wait_recv()
                z_put(left_t, p, gr[left_t, p * piece:(p + 1) * piece, :] + z_received(left_t, p))
                sum_left(left_t, p).start()

        return carry

    lax.fori_loop(0, 2 * n, pass_on, 0)

    a_copy(1).wait_recv()
    gl_out[...] = gl[off] + arecv[1].astype(jnp.float32) * arecv_s[1]
    b_copy().wait_recv()
    gl_out[...] += brecv[...].astype(jnp.float32) * brecv_s[...]

    for p in range(PIECES):
        span = slice(p * piece, (p + 1) * piece)

        @pl.when(has_l)
        def _(p=p, span=span):
            sum_arrived(me, p).wait_recv()
            gr[me, span, :] += z_received(me, p)

        @pl.when(has_r)
        def _(p=p, span=span):
            sum_arrived(n, p).wait_recv()
            gr[me, span, :] += z_received(n, p)

        gr_out[:, span] = gr[me, span, :].T

    left_copy(off, cross, 1).wait_send()
    left_copy(off, sib, 0).wait_send()
    left_copy(cross, sib, 2).wait_send()
    for which in range(2):
        a_copy(which).wait_send()
    b_copy().wait_send()

    def drain(t, carry):
        @pl.when(has_r & (t <= me))
        def _():
            gather_right(t).wait_send()

        @pl.when(has_l & (t >= me))
        def _():
            gather_left(t).wait_send()

        @pl.when(t > me)
        def _():
            for p in range(PIECES):
                sum_right(t, p).wait_send()

        @pl.when(t < me)
        def _():
            for p in range(PIECES):
                sum_left(t, p).wait_send()

        return carry

    lax.fori_loop(0, n, drain, 0)


def kernel_device(n, observed, trace_mask, left_factor, right_factor):
    rb, k = left_factor.shape[1:]
    n_off = 4
    rows = rb * n_off
    tr = min(256, rb)
    tiles = rows // tr
    dma = pltpu.SemaphoreType.DMA
    any_spec = pl.BlockSpec(memory_space=pl.ANY)
    vmem_spec = pl.BlockSpec(memory_space=pltpu.VMEM)
    bf16, f32 = jnp.bfloat16, jnp.float32
    left_share, right_share = pl.pallas_call(
        lambda *refs: kernel(n, rb, k, tr, *refs),
        out_shape=[
            jax.ShapeDtypeStruct((rb, 2 * k), f32),
            jax.ShapeDtypeStruct((rb, 2 * k), f32),
        ],
        in_specs=[any_spec] * 4,
        out_specs=[vmem_spec] * 2,
        scratch_shapes=[
            pltpu.VMEM((n_off, rb, 2 * k), bf16),
            pltpu.VMEM((n, rb, 2 * k), bf16),
            pltpu.VMEM((2 * rb, 2 * k), bf16),
            pltpu.VMEM((tiles, 2 * k, 2 * tr), bf16),
            pltpu.VMEM((2, 2, rows, rb), bf16),
            pltpu.VMEM((2, rows, rb), jnp.int32),
            pltpu.VMEM((n_off, rb, 2 * k), f32),
            pltpu.VMEM((n, 2 * k, rb), f32),
            pltpu.VMEM((n, PIECES, 2 * k // PIECES, rb), LINK),
            pltpu.VMEM((n + 1, PIECES, 2 * k // PIECES, rb), LINK),
            pltpu.VMEM((2, rb, 2 * k), LINK),
            pltpu.VMEM((2, rb, 2 * k), LINK),
            pltpu.VMEM((rb, 2 * k), LINK),
            pltpu.VMEM((rb, 2 * k), LINK),
            pltpu.VMEM((n, PIECES, 1, rb), f32),
            pltpu.VMEM((n + 1, PIECES, 1, rb), f32),
            pltpu.VMEM((2, 1, 2 * k), f32),
            pltpu.VMEM((2, 1, 2 * k), f32),
            pltpu.VMEM((1, 2 * k), f32),
            pltpu.VMEM((1, 2 * k), f32),
            dma((4,)), dma((2,)), dma((2,)),
            dma((n,)), dma((n,)), dma((n,)),
            dma((3,)), dma((3,)),
            dma((n, PIECES)), dma((n + 1, PIECES)),
            dma((2,)), dma((2,)), dma(()), dma(()),
            dma((n, PIECES)), dma((n + 1, PIECES)),
            dma((2,)), dma((2,)), dma(()), dma(()),
        ],
        compiler_params=pltpu.CompilerParams(
            collective_id=0, has_side_effects=True, vmem_limit_bytes=60 * 1024 * 1024),
        cost_estimate=pl.CostEstimate(
            flops=24 * rows * n * rb * k, bytes_accessed=8 * rows * n * rb, transcendentals=0),
    )(observed, trace_mask, left_factor, right_factor)
    left_share = jnp.stack([left_share[:, :k], left_share[:, k:]])
    right_share = jnp.stack([right_share[:, :k], right_share[:, k:]])
    left_next = left_factor.astype(f32) - STEP * left_share
    right_next = right_factor.astype(f32) - STEP * right_share
    return (left_next, right_next)


def solution(mesh):
    n, n_off = mesh.shape["mid"], mesh.shape["off"]

    def per_device(observed, trace_mask, left_factor, right_factor):
        rb, k = left_factor.shape[1:]
        if n_off == 4 and 2 <= n <= 4 and rb % 256 == 0 and rb <= 512 and k == 256:
            return kernel_device(n, observed, trace_mask, left_factor, right_factor)
        return plain_device(observed, trace_mask, left_factor, right_factor)

    in_specs = (
        P("freq", "mid", "off"),
        P("mid", "off"),
        P("freq", ("mid", "off"), None),
        P("freq", ("off", "mid"), None),
    )
    out_specs = (P("freq", ("mid", "off"), None), P("freq", ("off", "mid"), None))
    return jax.shard_map(
        per_device, mesh=mesh, in_specs=in_specs, out_specs=out_specs, check_vma=False
    )
```

```python
import math

import jax
import jax.numpy as jnp
from jax import lax
from jax.experimental import pallas as pl
from jax.experimental.pallas import tpu as pltpu
from jax.sharding import PartitionSpec as P

N = 8192
STEP = 2.0 / math.sqrt(N)
LINK = jnp.int16
LEVELS = 32000.0
PIECES = 8
MESH = pl.DeviceIdType.MESH


def outer_rows(first, second):
    return jnp.einsum("ik,jk->ij", first, second, preferred_element_type=jnp.float32)


def inner_rows(first, second):
    return jnp.einsum("ij,jk->ik", first, second, preferred_element_type=jnp.float32)


def inner_cols(first, second):
    return jnp.einsum("ij,ik->jk", first, second, preferred_element_type=jnp.float32)


def plain_device(observed, trace_mask, left_factor, right_factor):
    left = lax.all_gather(left_factor, "off", axis=1, tiled=True)
    keep = trace_mask.astype(jnp.float32)
    right = lax.all_gather(right_factor, "mid", axis=1, tiled=True)
    real_part = outer_rows(left[0], right[0]) + outer_rows(left[1], right[1])
    imag_part = outer_rows(left[1], right[0]) - outer_rows(left[0], right[1])
    miss_re = (keep * (real_part - observed[0].astype(jnp.float32))).astype(jnp.bfloat16)
    miss_im = (keep * (imag_part - observed[1].astype(jnp.float32))).astype(jnp.bfloat16)
    grad_left = jnp.stack(
        [
            inner_rows(miss_re, right[0]) - inner_rows(miss_im, right[1]),
            inner_rows(miss_re, right[1]) + inner_rows(miss_im, right[0]),
        ]
    )
    grad_right = jnp.stack(
        [
            inner_cols(miss_re, left[0]) + inner_cols(miss_im, left[1]),
            inner_cols(miss_re, left[1]) - inner_cols(miss_im, left[0]),
        ]
    )
    right_share = lax.psum_scatter(grad_right, "mid", scatter_dimension=1, tiled=True)
    left_share = lax.psum_scatter(grad_left, "off", scatter_dimension=1, tiled=True)
    left_next = left_factor.astype(jnp.float32) - STEP * left_share
    right_next = right_factor.astype(jnp.float32) - STEP * right_share
    return (left_next, right_next)


def coded(value):
    top = jnp.maximum(jnp.max(jnp.abs(value), axis=0, keepdims=True), 1e-30)
    levels = jnp.floor(value * (LEVELS / top) + 0.5)
    return levels.astype(jnp.int32).astype(LINK), top * (1.0 / LEVELS)


class Both:
    def __init__(self, *copies):
        self.copies = copies

    def start(self):
        for c in self.copies:
            c.start()

    def wait_recv(self):
        for c in self.copies:
            c.wait_recv()

    def wait_send(self):
        for c in self.copies:
            c.wait_send()


def kernel(
    n, rb, k, tr,
    obs_hbm, mask_hbm, left_hbm, right_hbm,
    gl_out, gr_out,
    lfull, rcat, rbig, lt, obs, mask, gl, gr,
    zsend, zrecv, asend, arecv, bsend, brecv,
    zsend_s, zrecv_s, asend_s, arecv_s, bsend_s, brecv_s,
    in_sem, obs_sem, mask_sem,
    g_send_r, g_send_l, g_recv,
    l_send, l_recv,
    z_send_sem, z_recv_sem,
    a_send_sem, a_recv_sem, b_send_sem, b_recv_sem,
    z_send_sem_s, z_recv_sem_s, a_send_sem_s, a_recv_sem_s, b_send_sem_s, b_recv_sem_s,
):
    me = lax.axis_index("mid")
    off = lax.axis_index("off")
    sib = off + 1 - 2 * lax.rem(off, 2)
    cross = lax.rem(off + 2, 4)
    diag = lax.rem(sib + 2, 4)
    lo = jnp.minimum(me, n - 1 - me)
    has_l = me > 0
    has_r = me < n - 1
    piece = 2 * k // PIECES
    tiles = rb // tr

    def block_at(j):
        near = (j + 1) // 2
        up = lax.rem(j, 2) == 1
        paired = jnp.where(up, me + near, me - near)
        far = j - lo
        single = jnp.where(me < n - 1 - me, me + far, me - far)
        return jnp.where(j <= 2 * lo, paired, single)

    def step_block(j):
        other = block_at(jnp.where(j == n, n - 1, j))
        return jnp.where((j == 0) | (j == n - 1), me, other)

    def row_block(q):
        return jnp.where(q == 0, off, jnp.where(q == 1, sib, jnp.where(q == 2, cross, diag)))

    def obs_copy(j):
        b = step_block(j)
        cols = pl.ds(pl.multiple_of(b * rb, rb), rb)
        slot = lax.rem(j, 2)
        return (
            pltpu.make_async_copy(obs_hbm.at[:, :, cols], obs.at[slot], obs_sem.at[slot]),
            pltpu.make_async_copy(mask_hbm.at[:, cols], mask.at[slot], mask_sem.at[slot]),
        )

    def gather_right(b):
        return pltpu.make_async_remote_copy(
            src_ref=rcat.at[b], dst_ref=rcat.at[b], send_sem=g_send_r.at[b], recv_sem=g_recv.at[b],
            device_id={"mid": jnp.minimum(me + 1, n - 1)}, device_id_type=MESH)

    def gather_left(b):
        return pltpu.make_async_remote_copy(
            src_ref=rcat.at[b], dst_ref=rcat.at[b], send_sem=g_send_l.at[b], recv_sem=g_recv.at[b],
            device_id={"mid": jnp.maximum(me - 1, 0)}, device_id_type=MESH)

    def left_copy(block, to, which):
        return pltpu.make_async_remote_copy(
            src_ref=lfull.at[block], dst_ref=lfull.at[block],
            send_sem=l_send.at[which], recv_sem=l_recv.at[which],
            device_id={"off": to}, device_id_type=MESH)

    def arrive(b):
        @pl.when(b < me)
        def _():
            gather_right(b).wait_recv()

            @pl.when(has_r)
            def _():
                gather_right(b).start()

        @pl.when(b > me)
        def _():
            gather_left(b).wait_recv()

            @pl.when(has_l)
            def _():
                gather_left(b).start()

    def sum_right(t, p):
        to = jnp.minimum(me + 1, n - 1)
        return Both(
            pltpu.make_async_remote_copy(
                src_ref=zsend.at[t, p], dst_ref=zrecv.at[t, p],
                send_sem=z_send_sem.at[t, p], recv_sem=z_recv_sem.at[t, p],
                device_id={"mid": to}, device_id_type=MESH),
            pltpu.make_async_remote_copy(
                src_ref=zsend_s.at[t, p], dst_ref=zrecv_s.at[t, p],
                send_sem=z_send_sem_s.at[t, p], recv_sem=z_recv_sem_s.at[t, p],
                device_id={"mid": to}, device_id_type=MESH))

    def sum_left(t, p):
        to = jnp.maximum(me - 1, 0)
        slot = jnp.where(t == me - 1, n, t)
        return Both(
            pltpu.make_async_remote_copy(
                src_ref=zsend.at[t, p], dst_ref=zrecv.at[slot, p],
                send_sem=z_send_sem.at[t, p], recv_sem=z_recv_sem.at[slot, p],
                device_id={"mid": to}, device_id_type=MESH),
            pltpu.make_async_remote_copy(
                src_ref=zsend_s.at[t, p], dst_ref=zrecv_s.at[slot, p],
                send_sem=z_send_sem_s.at[t, p], recv_sem=z_recv_sem_s.at[slot, p],
                device_id={"mid": to}, device_id_type=MESH))

    def sum_arrived(slot, p):
        return Both(
            pltpu.make_async_remote_copy(
                src_ref=zrecv.at[slot, p], dst_ref=zrecv.at[slot, p],
                send_sem=z_send_sem.at[0, p], recv_sem=z_recv_sem.at[slot, p],
                device_id={"off": sib}, device_id_type=MESH),
            pltpu.make_async_remote_copy(
                src_ref=zrecv_s.at[slot, p], dst_ref=zrecv_s.at[slot, p],
                send_sem=z_send_sem_s.at[0, p], recv_sem=z_recv_sem_s.at[slot, p],
                device_id={"off": sib}, device_id_type=MESH))

    def a_copy(which):
        return Both(
            pltpu.make_async_remote_copy(
                src_ref=asend.at[which], dst_ref=arecv.at[which],
                send_sem=a_send_sem.at[which], recv_sem=a_recv_sem.at[which],
                device_id={"off": sib}, device_id_type=MESH),
            pltpu.make_async_remote_copy(
                src_ref=asend_s.at[which], dst_ref=arecv_s.at[which],
                send_sem=a_send_sem_s.at[which], recv_sem=a_recv_sem_s.at[which],
                device_id={"off": sib}, device_id_type=MESH))

    def b_copy():
        return Both(
            pltpu.make_async_remote_copy(
                src_ref=bsend, dst_ref=brecv, send_sem=b_send_sem, recv_sem=b_recv_sem,
                device_id={"off": cross}, device_id_type=MESH),
            pltpu.make_async_remote_copy(
                src_ref=bsend_s, dst_ref=brecv_s, send_sem=b_send_sem_s, recv_sem=b_recv_sem_s,
                device_id={"off": cross}, device_id_type=MESH))

    def z_received(slot, p):
        return zrecv[slot, p].astype(jnp.float32) * zrecv_s[slot, p]

    def z_put(t, p, value):
        zsend[t, p], zsend_s[t, p] = coded(value)

    own = [
        pltpu.make_async_copy(left_hbm.at[0], lfull.at[off, :, 0:k], in_sem.at[0]),
        pltpu.make_async_copy(left_hbm.at[1], lfull.at[off, :, k:2 * k], in_sem.at[1]),
        pltpu.make_async_copy(right_hbm.at[0], rcat.at[me, :, 0:k], in_sem.at[2]),
        pltpu.make_async_copy(right_hbm.at[1], rcat.at[me, :, k:2 * k], in_sem.at[3]),
    ]
    for c in own:
        c.start()
    for c in obs_copy(0):
        c.start()

    barrier = pltpu.get_barrier_semaphore()
    for to in (sib, cross):
        pl.semaphore_signal(barrier, inc=1, device_id={"off": to}, device_id_type=MESH)

    @pl.when(has_l)
    def _():
        pl.semaphore_signal(barrier, inc=1, device_id={"mid": me - 1}, device_id_type=MESH)

    @pl.when(has_r)
    def _():
        pl.semaphore_signal(barrier, inc=1, device_id={"mid": me + 1}, device_id_type=MESH)

    pl.semaphore_wait(barrier, 2 + jnp.where(has_l, 1, 0) + jnp.where(has_r, 1, 0))

    for c in own:
        c.wait()

    left_copy(off, cross, 1).start()
    left_copy(off, sib, 0).start()

    @pl.when(has_r)
    def _():
        gather_right(me).start()

    @pl.when(has_l)
    def _():
        gather_left(me).start()

    gl[...] = jnp.zeros_like(gl)

    middle = has_l & has_r

    def arrive_group(nxt):
        pair = (nxt <= 2 * lo) & (lax.rem(nxt, 2) == 1)

        @pl.when(pair)
        def _():
            near = (nxt + 1) // 2
            arrive(me + near)
            arrive(me - near)

        @pl.when(nxt > 2 * lo)
        def _():
            arrive(block_at(nxt))

    def step(j, carry):
        b = step_block(j)
        slot = lax.rem(j, 2)
        first, late, last = j == 0, j == n - 1, j == n

        @pl.when(j < n)
        def _():
            for c in obs_copy(j + 1):
                c.start()

        @pl.when(j == 1)
        def _():
            left_copy(cross, cross, 1).wait_recv()
            left_copy(cross, sib, 2).start()

        @pl.when(jnp.logical_not(middle | first | late))
        def _():
            arrive(b)

        rbig[0:rb, :] = rcat[b]
        rbig[rb:2 * rb, 0:k] = -rcat[b, :, k:2 * k]
        rbig[rb:2 * rb, k:2 * k] = rcat[b, :, 0:k]

        @pl.when(jnp.logical_not(late))
        def _():
            gr[b] = jnp.zeros(gr.shape[1:], jnp.float32)

        for c in obs_copy(j):
            c.wait()

        def rows(i, carry):
            q_of = i // tiles
            t = lax.rem(i, tiles)
            q = jnp.where(last, 3 - q_of, jnp.where(late, 2 + q_of, q_of))
            block = row_block(q)

            @pl.when((t == 0) & first & (q == 1))
            def _():
                left_copy(sib, sib, 0).wait_recv()

            @pl.when((t == 0) & (j == 1) & (q == 3))
            def _():
                left_copy(diag, sib, 2).wait_recv()

            @pl.when(middle & (j >= 1) & (j <= n - 2) & (i == 2 * tiles))
            def _():
                arrive_group(j + 1)

            at = pl.ds(pl.multiple_of(t * tr, tr), tr)
            row_at = pl.ds(pl.multiple_of(block * rb + t * tr, tr), tr)
            lrows = lfull[block, at, :]

            @pl.when(first | ((j == 1) & (q >= 2)))
            def _():
                turned = lrows.astype(jnp.float32).T.astype(jnp.bfloat16)
                lt[block * tiles + t, :, 0:tr] = turned
                lt[block * tiles + t, 0:k, tr:2 * tr] = turned[k:2 * k]
                lt[block * tiles + t, k:2 * k, tr:2 * tr] = -turned[0:k]

            pred = lax.dot_general(
                lrows, rbig[...], (((1,), (1,)), ((), ())), preferred_element_type=jnp.float32)
            keep = mask[slot, row_at, :] != 0
            miss_re = jnp.where(
                keep, pred[:, 0:rb] - obs[slot, 0, row_at, :].astype(jnp.float32), 0.0
            ).astype(jnp.bfloat16)
            miss_im = jnp.where(
                keep, pred[:, rb:2 * rb] - obs[slot, 1, row_at, :].astype(jnp.float32), 0.0
            ).astype(jnp.bfloat16)
            gl[block, at, :] += jnp.dot(
                jnp.concatenate([miss_re, miss_im], axis=1), rbig[...],
                preferred_element_type=jnp.float32)
            gr[b] += jnp.dot(
                lt[block * tiles + t], jnp.concatenate([miss_re, miss_im], axis=0),
                preferred_element_type=jnp.float32)

            @pl.when(last & (t == tiles - 1))
            def _():
                @pl.when(q == 3)
                def _():
                    asend[0], asend_s[0] = coded(gl[diag])
                    a_copy(0).start()

                @pl.when(q == 1)
                def _():
                    asend[1], asend_s[1] = coded(gl[sib])
                    a_copy(1).start()
                    a_copy(0).wait_recv()
                    bsend[...], bsend_s[...] = coded(
                        gl[cross] + arecv[0].astype(jnp.float32) * arecv_s[0])
                    b_copy().start()

            return carry

        lax.fori_loop(0, jnp.where(first | late, 2 * tiles, 4 * tiles), rows, 0)

        @pl.when(middle & first)
        def _():
            arrive_group(1)

        @pl.when(jnp.logical_and(me == 0, b > me))
        def _():
            for p in range(PIECES):
                z_put(b, p, gr[b, p * piece:(p + 1) * piece, :])
                sum_right(b, p).start()

        @pl.when(jnp.logical_and(me == n - 1, b < me))
        def _():
            for p in range(PIECES):
                z_put(b, p, gr[b, p * piece:(p + 1) * piece, :])
                sum_left(b, p).start()

        return carry

    lax.fori_loop(0, n + 1, step, 0)

    def pass_on(tau, carry):
        right_t = tau - me
        left_t = 2 * (n - 1) - me - tau

        @pl.when((me > 0) & (right_t > me) & (right_t < n))
        def _():
            for p in range(PIECES):
                sum_arrived(right_t, p).wait_recv()
                z_put(right_t, p, gr[right_t, p * piece:(p + 1) * piece, :] + z_received(right_t, p))
                sum_right(right_t, p).start()

        @pl.when((me < n - 1) & (left_t < me) & (left_t >= 0))
        def _():
            for p in range(PIECES):
                sum_arrived(left_t, p).wait_recv()
                z_put(left_t, p, gr[left_t, p * piece:(p + 1) * piece, :] + z_received(left_t, p))
                sum_left(left_t, p).start()

        return carry

    lax.fori_loop(0, 2 * n, pass_on, 0)

    a_copy(1).wait_recv()
    gl[off] += arecv[1].astype(jnp.float32) * arecv_s[1]
    b_copy().wait_recv()
    for c in range(2):
        part = slice(c * k, (c + 1) * k)
        total = gl[off, :, part] + brecv[:, part].astype(jnp.float32) * brecv_s[:, part]
        gl_out[c] = lfull[off, :, part].astype(jnp.float32) - STEP * total

    for p in range(PIECES):
        span = slice(p * piece, (p + 1) * piece)

        @pl.when(has_l)
        def _(p=p, span=span):
            sum_arrived(me, p).wait_recv()
            gr[me, span, :] += z_received(me, p)

        @pl.when(has_r)
        def _(p=p, span=span):
            sum_arrived(n, p).wait_recv()
            gr[me, span, :] += z_received(n, p)

        if (p + 1) * piece % 128 == 0:
            low = (p + 1) * piece - 128
            c, at = low // k, slice(low % k, low % k + 128)
            gr_out[c, :, at] = (
                rcat[me, :, low:low + 128].astype(jnp.float32) - STEP * gr[me, low:low + 128, :].T)

    left_copy(off, cross, 1).wait_send()
    left_copy(off, sib, 0).wait_send()
    left_copy(cross, sib, 2).wait_send()
    for which in range(2):
        a_copy(which).wait_send()
    b_copy().wait_send()

    def drain(t, carry):
        @pl.when(has_r & (t <= me))
        def _():
            gather_right(t).wait_send()

        @pl.when(has_l & (t >= me))
        def _():
            gather_left(t).wait_send()

        @pl.when(t > me)
        def _():
            for p in range(PIECES):
                sum_right(t, p).wait_send()

        @pl.when(t < me)
        def _():
            for p in range(PIECES):
                sum_left(t, p).wait_send()

        return carry

    lax.fori_loop(0, n, drain, 0)


def kernel_device(n, observed, trace_mask, left_factor, right_factor):
    rb, k = left_factor.shape[1:]
    n_off = 4
    rows = rb * n_off
    tr = rb
    tiles = rows // tr
    dma = pltpu.SemaphoreType.DMA
    any_spec = pl.BlockSpec(memory_space=pl.ANY)
    vmem_spec = pl.BlockSpec(memory_space=pltpu.VMEM)
    bf16, f32 = jnp.bfloat16, jnp.float32
    return pl.pallas_call(
        lambda *refs: kernel(n, rb, k, tr, *refs),
        out_shape=[
            jax.ShapeDtypeStruct((2, rb, k), f32),
            jax.ShapeDtypeStruct((2, rb, k), f32),
        ],
        in_specs=[any_spec] * 4,
        out_specs=[vmem_spec] * 2,
        scratch_shapes=[
            pltpu.VMEM((n_off, rb, 2 * k), bf16),
            pltpu.VMEM((n, rb, 2 * k), bf16),
            pltpu.VMEM((2 * rb, 2 * k), bf16),
            pltpu.VMEM((tiles, 2 * k, 2 * tr), bf16),
            pltpu.VMEM((2, 2, rows, rb), bf16),
            pltpu.VMEM((2, rows, rb), jnp.int32),
            pltpu.VMEM((n_off, rb, 2 * k), f32),
            pltpu.VMEM((n, 2 * k, rb), f32),
            pltpu.VMEM((n, PIECES, 2 * k // PIECES, rb), LINK),
            pltpu.VMEM((n + 1, PIECES, 2 * k // PIECES, rb), LINK),
            pltpu.VMEM((2, rb, 2 * k), LINK),
            pltpu.VMEM((2, rb, 2 * k), LINK),
            pltpu.VMEM((rb, 2 * k), LINK),
            pltpu.VMEM((rb, 2 * k), LINK),
            pltpu.VMEM((n, PIECES, 1, rb), f32),
            pltpu.VMEM((n + 1, PIECES, 1, rb), f32),
            pltpu.VMEM((2, 1, 2 * k), f32),
            pltpu.VMEM((2, 1, 2 * k), f32),
            pltpu.VMEM((1, 2 * k), f32),
            pltpu.VMEM((1, 2 * k), f32),
            dma((4,)), dma((2,)), dma((2,)),
            dma((n,)), dma((n,)), dma((n,)),
            dma((3,)), dma((3,)),
            dma((n, PIECES)), dma((n + 1, PIECES)),
            dma((2,)), dma((2,)), dma(()), dma(()),
            dma((n, PIECES)), dma((n + 1, PIECES)),
            dma((2,)), dma((2,)), dma(()), dma(()),
        ],
        compiler_params=pltpu.CompilerParams(
            collective_id=0, has_side_effects=True, vmem_limit_bytes=60 * 1024 * 1024),
        cost_estimate=pl.CostEstimate(
            flops=24 * rows * n * rb * k, bytes_accessed=8 * rows * n * rb, transcendentals=0),
    )(observed, trace_mask, left_factor, right_factor)


def solution(mesh):
    n, n_off = mesh.shape["mid"], mesh.shape["off"]

    def per_device(observed, trace_mask, left_factor, right_factor):
        rb, k = left_factor.shape[1:]
        if n_off == 4 and 2 <= n <= 4 and rb % 256 == 0 and rb <= 512 and k == 256:
            return kernel_device(n, observed, trace_mask, left_factor, right_factor)
        return plain_device(observed, trace_mask, left_factor, right_factor)

    in_specs = (
        P("freq", "mid", "off"),
        P("mid", "off"),
        P("freq", ("mid", "off"), None),
        P("freq", ("off", "mid"), None),
    )
    out_specs = (P("freq", ("mid", "off"), None), P("freq", ("off", "mid"), None))
    return jax.shard_map(
        per_device, mesh=mesh, in_specs=in_specs, out_specs=out_specs, check_vma=False
    )
```

```python
import math

import jax
import jax.numpy as jnp
from jax import lax
from jax.experimental import pallas as pl
from jax.experimental.pallas import tpu as pltpu
from jax.sharding import PartitionSpec as P

N = 8192
STEP = 2.0 / math.sqrt(N)
LINK = jnp.int16
LEVELS = 32000.0
PIECES = 8
MESH = pl.DeviceIdType.MESH


def outer_rows(first, second):
    return jnp.einsum("ik,jk->ij", first, second, preferred_element_type=jnp.float32)


def inner_rows(first, second):
    return jnp.einsum("ij,jk->ik", first, second, preferred_element_type=jnp.float32)


def inner_cols(first, second):
    return jnp.einsum("ij,ik->jk", first, second, preferred_element_type=jnp.float32)


def plain_device(observed, trace_mask, left_factor, right_factor):
    left = lax.all_gather(left_factor, "off", axis=1, tiled=True)
    keep = trace_mask.astype(jnp.float32)
    right = lax.all_gather(right_factor, "mid", axis=1, tiled=True)
    real_part = outer_rows(left[0], right[0]) + outer_rows(left[1], right[1])
    imag_part = outer_rows(left[1], right[0]) - outer_rows(left[0], right[1])
    miss_re = (keep * (real_part - observed[0].astype(jnp.float32))).astype(jnp.bfloat16)
    miss_im = (keep * (imag_part - observed[1].astype(jnp.float32))).astype(jnp.bfloat16)
    grad_left = jnp.stack(
        [
            inner_rows(miss_re, right[0]) - inner_rows(miss_im, right[1]),
            inner_rows(miss_re, right[1]) + inner_rows(miss_im, right[0]),
        ]
    )
    grad_right = jnp.stack(
        [
            inner_cols(miss_re, left[0]) + inner_cols(miss_im, left[1]),
            inner_cols(miss_re, left[1]) - inner_cols(miss_im, left[0]),
        ]
    )
    right_share = lax.psum_scatter(grad_right, "mid", scatter_dimension=1, tiled=True)
    left_share = lax.psum_scatter(grad_left, "off", scatter_dimension=1, tiled=True)
    left_next = left_factor.astype(jnp.float32) - STEP * left_share
    right_next = right_factor.astype(jnp.float32) - STEP * right_share
    return (left_next, right_next)


def coded(value):
    top = jnp.maximum(jnp.max(jnp.abs(value), axis=0, keepdims=True), 1e-30)
    levels = jnp.floor(value * (LEVELS / top) + 0.5)
    return levels.astype(jnp.int32).astype(LINK), top * (1.0 / LEVELS)


class Both:
    def __init__(self, *copies):
        self.copies = copies

    def start(self):
        for c in self.copies:
            c.start()

    def wait_recv(self):
        for c in self.copies:
            c.wait_recv()

    def wait_send(self):
        for c in self.copies:
            c.wait_send()


def kernel(
    n, rb, k, tr,
    obs_hbm, mask_hbm, left_hbm, right_hbm,
    gl_out, gr_out,
    lfull, rcat, rbig, lt, obs, mask, gl, gr,
    zsend, zrecv, asend, arecv, bsend, brecv,
    zsend_s, zrecv_s, asend_s, arecv_s, bsend_s, brecv_s,
    in_sem, obs_sem, mask_sem,
    g_send_r, g_send_l, g_recv,
    l_send, l_recv,
    z_send_sem, z_recv_sem,
    a_send_sem, a_recv_sem, b_send_sem, b_recv_sem,
    z_send_sem_s, z_recv_sem_s, a_send_sem_s, a_recv_sem_s, b_send_sem_s, b_recv_sem_s,
):
    me = lax.axis_index("mid")
    off = lax.axis_index("off")
    sib = off + 1 - 2 * lax.rem(off, 2)
    cross = lax.rem(off + 2, 4)
    diag = lax.rem(sib + 2, 4)
    lo = jnp.minimum(me, n - 1 - me)
    has_l = me > 0
    has_r = me < n - 1
    piece = 2 * k // PIECES
    tiles = rb // tr

    def block_at(j):
        near = (j + 1) // 2
        up = lax.rem(j, 2) == 1
        paired = jnp.where(up, me + near, me - near)
        far = j - lo
        single = jnp.where(me < n - 1 - me, me + far, me - far)
        return jnp.where(j <= 2 * lo, paired, single)

    def step_block(j):
        other = block_at(jnp.where(j == n, n - 1, j))
        return jnp.where((j == 0) | (j == n - 1), me, other)

    def row_block(q):
        return jnp.where(q == 0, off, jnp.where(q == 1, sib, jnp.where(q == 2, cross, diag)))

    def obs_copy(j):
        b = step_block(j)
        cols = pl.ds(pl.multiple_of(b * rb, rb), rb)
        slot = lax.rem(j, 2)
        return (
            pltpu.make_async_copy(obs_hbm.at[:, :, cols], obs.at[slot], obs_sem.at[slot]),
            pltpu.make_async_copy(mask_hbm.at[:, cols], mask.at[slot], mask_sem.at[slot]),
        )

    def gather_right(b):
        return pltpu.make_async_remote_copy(
            src_ref=rcat.at[b], dst_ref=rcat.at[b], send_sem=g_send_r.at[b], recv_sem=g_recv.at[b],
            device_id={"mid": jnp.minimum(me + 1, n - 1)}, device_id_type=MESH)

    def gather_left(b):
        return pltpu.make_async_remote_copy(
            src_ref=rcat.at[b], dst_ref=rcat.at[b], send_sem=g_send_l.at[b], recv_sem=g_recv.at[b],
            device_id={"mid": jnp.maximum(me - 1, 0)}, device_id_type=MESH)

    def left_copy(block, to, which):
        return pltpu.make_async_remote_copy(
            src_ref=lfull.at[block], dst_ref=lfull.at[block],
            send_sem=l_send.at[which], recv_sem=l_recv.at[which],
            device_id={"off": to}, device_id_type=MESH)

    def arrive(b):
        @pl.when(b < me)
        def _():
            gather_right(b).wait_recv()

            @pl.when(has_r)
            def _():
                gather_right(b).start()

        @pl.when(b > me)
        def _():
            gather_left(b).wait_recv()

            @pl.when(has_l)
            def _():
                gather_left(b).start()

    def sum_right(t, p):
        to = jnp.minimum(me + 1, n - 1)
        return Both(
            pltpu.make_async_remote_copy(
                src_ref=zsend.at[t, p], dst_ref=zrecv.at[t, p],
                send_sem=z_send_sem.at[t, p], recv_sem=z_recv_sem.at[t, p],
                device_id={"mid": to}, device_id_type=MESH),
            pltpu.make_async_remote_copy(
                src_ref=zsend_s.at[t, p], dst_ref=zrecv_s.at[t, p],
                send_sem=z_send_sem_s.at[t, p], recv_sem=z_recv_sem_s.at[t, p],
                device_id={"mid": to}, device_id_type=MESH))

    def sum_left(t, p):
        to = jnp.maximum(me - 1, 0)
        slot = jnp.where(t == me - 1, n, t)
        return Both(
            pltpu.make_async_remote_copy(
                src_ref=zsend.at[t, p], dst_ref=zrecv.at[slot, p],
                send_sem=z_send_sem.at[t, p], recv_sem=z_recv_sem.at[slot, p],
                device_id={"mid": to}, device_id_type=MESH),
            pltpu.make_async_remote_copy(
                src_ref=zsend_s.at[t, p], dst_ref=zrecv_s.at[slot, p],
                send_sem=z_send_sem_s.at[t, p], recv_sem=z_recv_sem_s.at[slot, p],
                device_id={"mid": to}, device_id_type=MESH))

    def sum_arrived(slot, p):
        return Both(
            pltpu.make_async_remote_copy(
                src_ref=zrecv.at[slot, p], dst_ref=zrecv.at[slot, p],
                send_sem=z_send_sem.at[0, p], recv_sem=z_recv_sem.at[slot, p],
                device_id={"off": sib}, device_id_type=MESH),
            pltpu.make_async_remote_copy(
                src_ref=zrecv_s.at[slot, p], dst_ref=zrecv_s.at[slot, p],
                send_sem=z_send_sem_s.at[0, p], recv_sem=z_recv_sem_s.at[slot, p],
                device_id={"off": sib}, device_id_type=MESH))

    def a_copy(which):
        return Both(
            pltpu.make_async_remote_copy(
                src_ref=asend.at[which], dst_ref=arecv.at[which],
                send_sem=a_send_sem.at[which], recv_sem=a_recv_sem.at[which],
                device_id={"off": sib}, device_id_type=MESH),
            pltpu.make_async_remote_copy(
                src_ref=asend_s.at[which], dst_ref=arecv_s.at[which],
                send_sem=a_send_sem_s.at[which], recv_sem=a_recv_sem_s.at[which],
                device_id={"off": sib}, device_id_type=MESH))

    def b_copy():
        return Both(
            pltpu.make_async_remote_copy(
                src_ref=bsend, dst_ref=brecv, send_sem=b_send_sem, recv_sem=b_recv_sem,
                device_id={"off": cross}, device_id_type=MESH),
            pltpu.make_async_remote_copy(
                src_ref=bsend_s, dst_ref=brecv_s, send_sem=b_send_sem_s, recv_sem=b_recv_sem_s,
                device_id={"off": cross}, device_id_type=MESH))

    def z_received(slot, p):
        return zrecv[slot, p].astype(jnp.float32) * zrecv_s[slot, p]

    def z_put(t, p, value):
        zsend[t, p], zsend_s[t, p] = coded(value)

    own = [
        pltpu.make_async_copy(left_hbm.at[0], lfull.at[off, :, 0:k], in_sem.at[0]),
        pltpu.make_async_copy(left_hbm.at[1], lfull.at[off, :, k:2 * k], in_sem.at[1]),
        pltpu.make_async_copy(right_hbm.at[0], rcat.at[me, :, 0:k], in_sem.at[2]),
        pltpu.make_async_copy(right_hbm.at[1], rcat.at[me, :, k:2 * k], in_sem.at[3]),
    ]
    for c in own:
        c.start()
    for c in obs_copy(0):
        c.start()

    barrier = pltpu.get_barrier_semaphore()
    for to in (sib, cross):
        pl.semaphore_signal(barrier, inc=1, device_id={"off": to}, device_id_type=MESH)

    @pl.when(has_l)
    def _():
        pl.semaphore_signal(barrier, inc=1, device_id={"mid": me - 1}, device_id_type=MESH)

    @pl.when(has_r)
    def _():
        pl.semaphore_signal(barrier, inc=1, device_id={"mid": me + 1}, device_id_type=MESH)

    pl.semaphore_wait(barrier, 2 + jnp.where(has_l, 1, 0) + jnp.where(has_r, 1, 0))

    for c in own:
        c.wait()

    left_copy(off, cross, 1).start()
    left_copy(off, sib, 0).start()

    @pl.when(has_r)
    def _():
        gather_right(me).start()

    @pl.when(has_l)
    def _():
        gather_left(me).start()

    gl[...] = jnp.zeros_like(gl)

    middle = has_l & has_r

    def arrive_group(nxt):
        pair = (nxt <= 2 * lo) & (lax.rem(nxt, 2) == 1)

        @pl.when(pair)
        def _():
            near = (nxt + 1) // 2
            arrive(me + near)
            arrive(me - near)

        @pl.when(nxt > 2 * lo)
        def _():
            arrive(block_at(nxt))

    def step(j, carry):
        b = step_block(j)
        slot = lax.rem(j, 2)
        first, late, last = j == 0, j == n - 1, j == n

        @pl.when(j < n)
        def _():
            for c in obs_copy(j + 1):
                c.start()

        @pl.when(j == 1)
        def _():
            left_copy(cross, cross, 1).wait_recv()
            left_copy(cross, sib, 2).start()

        @pl.when(jnp.logical_not(middle | first | late))
        def _():
            arrive(b)

        rbig[0:rb, :] = rcat[b]
        rbig[rb:2 * rb, 0:k] = -rcat[b, :, k:2 * k]
        rbig[rb:2 * rb, k:2 * k] = rcat[b, :, 0:k]

        @pl.when(jnp.logical_not(late))
        def _():
            gr[b] = jnp.zeros(gr.shape[1:], jnp.float32)

        for c in obs_copy(j):
            c.wait()

        def rows(i, carry):
            q_of = i // tiles
            t = lax.rem(i, tiles)
            q = jnp.where(last, 3 - q_of, jnp.where(late, 2 + q_of, q_of))
            block = row_block(q)

            @pl.when((t == 0) & first & (q == 1))
            def _():
                left_copy(sib, sib, 0).wait_recv()

            @pl.when((t == 0) & (j == 1) & (q == 3))
            def _():
                left_copy(diag, sib, 2).wait_recv()

            @pl.when(middle & (j >= 1) & (j <= n - 2) & (i == 2 * tiles))
            def _():
                arrive_group(j + 1)

            at = pl.ds(pl.multiple_of(t * tr, tr), tr)
            row_at = pl.ds(pl.multiple_of(block * rb + t * tr, tr), tr)
            lrows = lfull[block, at, :]

            @pl.when(first | ((j == 1) & (q >= 2)))
            def _():
                turned = lrows.astype(jnp.float32).T.astype(jnp.bfloat16)
                lt[block * tiles + t, :, 0:tr] = turned
                lt[block * tiles + t, 0:k, tr:2 * tr] = turned[k:2 * k]
                lt[block * tiles + t, k:2 * k, tr:2 * tr] = -turned[0:k]

            pred = lax.dot_general(
                lrows, rbig[...], (((1,), (1,)), ((), ())), preferred_element_type=jnp.float32)
            keep = mask[slot, row_at, :] != 0
            miss_re = jnp.where(
                keep, pred[:, 0:rb] - obs[slot, 0, row_at, :].astype(jnp.float32), 0.0
            ).astype(jnp.bfloat16)
            miss_im = jnp.where(
                keep, pred[:, rb:2 * rb] - obs[slot, 1, row_at, :].astype(jnp.float32), 0.0
            ).astype(jnp.bfloat16)
            gl[block, at, :] += jnp.dot(
                jnp.concatenate([miss_re, miss_im], axis=1), rbig[...],
                preferred_element_type=jnp.float32)
            gr[b] += jnp.dot(
                lt[block * tiles + t], jnp.concatenate([miss_re, miss_im], axis=0),
                preferred_element_type=jnp.float32)

            @pl.when(last & (t == tiles - 1))
            def _():
                @pl.when(q == 3)
                def _():
                    asend[0], asend_s[0] = coded(gl[diag])
                    a_copy(0).start()

                @pl.when(q == 1)
                def _():
                    asend[1], asend_s[1] = coded(gl[sib])
                    a_copy(1).start()
                    a_copy(0).wait_recv()
                    bsend[...], bsend_s[...] = coded(
                        gl[cross] + arecv[0].astype(jnp.float32) * arecv_s[0])
                    b_copy().start()

            return carry

        lax.fori_loop(0, jnp.where(first | late, 2 * tiles, 4 * tiles), rows, 0)

        @pl.when(middle & first)
        def _():
            arrive_group(1)

        @pl.when(jnp.logical_and(me == 0, b > me))
        def _():
            for p in range(PIECES):
                z_put(b, p, gr[b, p * piece:(p + 1) * piece, :])
                sum_right(b, p).start()

        @pl.when(jnp.logical_and(me == n - 1, b < me))
        def _():
            for p in range(PIECES):
                z_put(b, p, gr[b, p * piece:(p + 1) * piece, :])
                sum_left(b, p).start()

        return carry

    lax.fori_loop(0, n + 1, step, 0)

    def pass_on(u, carry):
        right_v = jnp.maximum(u - me, 0)
        left_v = jnp.maximum(u - (n - 1 - me), 0)
        right_t, right_p = right_v // PIECES, lax.rem(right_v, PIECES)
        left_t, left_p = n - 1 - left_v // PIECES, lax.rem(left_v, PIECES)

        @pl.when((me > 0) & (u >= me) & (right_t > me) & (right_t < n))
        def _():
            sum_arrived(right_t, right_p).wait_recv()
            span = pl.ds(pl.multiple_of(right_p * piece, piece), piece)
            z_put(right_t, right_p, gr[right_t, span, :] + z_received(right_t, right_p))
            sum_right(right_t, right_p).start()

        @pl.when((me < n - 1) & (u >= n - 1 - me) & (left_t < me) & (left_t >= 0))
        def _():
            sum_arrived(left_t, left_p).wait_recv()
            span = pl.ds(pl.multiple_of(left_p * piece, piece), piece)
            z_put(left_t, left_p, gr[left_t, span, :] + z_received(left_t, left_p))
            sum_left(left_t, left_p).start()

        return carry

    lax.fori_loop(0, n * PIECES + n, pass_on, 0)

    a_copy(1).wait_recv()
    gl[off] += arecv[1].astype(jnp.float32) * arecv_s[1]
    b_copy().wait_recv()
    for c in range(2):
        part = slice(c * k, (c + 1) * k)
        total = gl[off, :, part] + brecv[:, part].astype(jnp.float32) * brecv_s[:, part]
        gl_out[c] = lfull[off, :, part].astype(jnp.float32) - STEP * total

    for p in range(PIECES):
        span = slice(p * piece, (p + 1) * piece)

        @pl.when(has_l)
        def _(p=p, span=span):
            sum_arrived(me, p).wait_recv()
            gr[me, span, :] += z_received(me, p)

        @pl.when(has_r)
        def _(p=p, span=span):
            sum_arrived(n, p).wait_recv()
            gr[me, span, :] += z_received(n, p)

        if (p + 1) * piece % 128 == 0:
            low = (p + 1) * piece - 128
            c, at = low // k, slice(low % k, low % k + 128)
            gr_out[c, :, at] = (
                rcat[me, :, low:low + 128].astype(jnp.float32) - STEP * gr[me, low:low + 128, :].T)

    left_copy(off, cross, 1).wait_send()
    left_copy(off, sib, 0).wait_send()
    left_copy(cross, sib, 2).wait_send()
    for which in range(2):
        a_copy(which).wait_send()
    b_copy().wait_send()

    def drain(t, carry):
        @pl.when(has_r & (t <= me))
        def _():
            gather_right(t).wait_send()

        @pl.when(has_l & (t >= me))
        def _():
            gather_left(t).wait_send()

        @pl.when(t > me)
        def _():
            for p in range(PIECES):
                sum_right(t, p).wait_send()

        @pl.when(t < me)
        def _():
            for p in range(PIECES):
                sum_left(t, p).wait_send()

        return carry

    lax.fori_loop(0, n, drain, 0)


def kernel_device(n, observed, trace_mask, left_factor, right_factor):
    rb, k = left_factor.shape[1:]
    n_off = 4
    rows = rb * n_off
    tr = rb
    tiles = rows // tr
    dma = pltpu.SemaphoreType.DMA
    any_spec = pl.BlockSpec(memory_space=pl.ANY)
    vmem_spec = pl.BlockSpec(memory_space=pltpu.VMEM)
    bf16, f32 = jnp.bfloat16, jnp.float32
    return pl.pallas_call(
        lambda *refs: kernel(n, rb, k, tr, *refs),
        out_shape=[
            jax.ShapeDtypeStruct((2, rb, k), f32),
            jax.ShapeDtypeStruct((2, rb, k), f32),
        ],
        in_specs=[any_spec] * 4,
        out_specs=[vmem_spec] * 2,
        scratch_shapes=[
            pltpu.VMEM((n_off, rb, 2 * k), bf16),
            pltpu.VMEM((n, rb, 2 * k), bf16),
            pltpu.VMEM((2 * rb, 2 * k), bf16),
            pltpu.VMEM((tiles, 2 * k, 2 * tr), bf16),
            pltpu.VMEM((2, 2, rows, rb), bf16),
            pltpu.VMEM((2, rows, rb), jnp.int32),
            pltpu.VMEM((n_off, rb, 2 * k), f32),
            pltpu.VMEM((n, 2 * k, rb), f32),
            pltpu.VMEM((n, PIECES, 2 * k // PIECES, rb), LINK),
            pltpu.VMEM((n + 1, PIECES, 2 * k // PIECES, rb), LINK),
            pltpu.VMEM((2, rb, 2 * k), LINK),
            pltpu.VMEM((2, rb, 2 * k), LINK),
            pltpu.VMEM((rb, 2 * k), LINK),
            pltpu.VMEM((rb, 2 * k), LINK),
            pltpu.VMEM((n, PIECES, 1, rb), f32),
            pltpu.VMEM((n + 1, PIECES, 1, rb), f32),
            pltpu.VMEM((2, 1, 2 * k), f32),
            pltpu.VMEM((2, 1, 2 * k), f32),
            pltpu.VMEM((1, 2 * k), f32),
            pltpu.VMEM((1, 2 * k), f32),
            dma((4,)), dma((2,)), dma((2,)),
            dma((n,)), dma((n,)), dma((n,)),
            dma((3,)), dma((3,)),
            dma((n, PIECES)), dma((n + 1, PIECES)),
            dma((2,)), dma((2,)), dma(()), dma(()),
            dma((n, PIECES)), dma((n + 1, PIECES)),
            dma((2,)), dma((2,)), dma(()), dma(()),
        ],
        compiler_params=pltpu.CompilerParams(
            collective_id=0, has_side_effects=True, vmem_limit_bytes=60 * 1024 * 1024),
        cost_estimate=pl.CostEstimate(
            flops=24 * rows * n * rb * k, bytes_accessed=8 * rows * n * rb, transcendentals=0),
    )(observed, trace_mask, left_factor, right_factor)


def solution(mesh):
    n, n_off = mesh.shape["mid"], mesh.shape["off"]

    def per_device(observed, trace_mask, left_factor, right_factor):
        rb, k = left_factor.shape[1:]
        if n_off == 4 and 2 <= n <= 4 and rb % 256 == 0 and rb <= 512 and k == 256:
            return kernel_device(n, observed, trace_mask, left_factor, right_factor)
        return plain_device(observed, trace_mask, left_factor, right_factor)

    in_specs = (
        P("freq", "mid", "off"),
        P("mid", "off"),
        P("freq", ("mid", "off"), None),
        P("freq", ("off", "mid"), None),
    )
    out_specs = (P("freq", ("mid", "off"), None), P("freq", ("off", "mid"), None))
    return jax.shard_map(
        per_device, mesh=mesh, in_specs=in_specs, out_specs=out_specs, check_vma=False
    )
```
